256 devices in a mesh: section: 16 (over x_hi, z), dp: 16 (over x_lo, y, core).
Axes of the slice: x: 4 (x_hi: 2, x_lo: 2; x = x_hi * 2 + x_lo), y: 4, z: 8, core: 2. Of those that a mesh axis runs over, the one named last changes fastest.
Arguments:
- grad_in: bfloat16 [16, 128, 8192], P('section', 'dp'), may hold values from -6 to 6
- weights: bfloat16 [16, 8192, 8192], P('section', 'dp'), may hold values from -0.0625 to 0.0625
- band_index: int32 [16, 8, 2], P('section'), may hold values from 0 to 15
- owner: int32 [16], replicated, may hold values from 0 to 15, each once
Outputs:
- factors: float32 [16, 16, 512, 512], P('section', 'dp')
- grad_out: bfloat16 [16, 128, 8192], P('section', 'dp')
The draws below stay inside these ranges and needn't reach their ends.
Inputs may be any that keep to these rules, and one draw needn't show every extreme that they name: `owner`: each slot number appears exactly once.
All inputs are finite; a program needn't handle non-finite values.
Results may differ from the reference program's by a relative error of at most 0.0051.
Values may be sent and summed in bfloat16 or wider, within the bound.
A program may use at most 128 MiB of HBM per device.

```python
import jax
import jax.numpy as jnp
from jax import lax

D = 8192
BLK = 512
NB = 8
STEPS = 2
TOKENS = 128
SECTIONS = 16


def place_ends(values, key, low, high):
    place = [jax.random.randint(jax.random.fold_in(key, axis), (), 0, length) for axis, length in enumerate(values.shape)]
    widest = values.shape.index(max(values.shape))
    next_to = place[:widest] + [(place[widest] + 1) % values.shape[widest]] + place[widest + 1:]
    return values.at[tuple(place)].set(low).at[tuple(next_to)].set(high)


def block_scale(own_key, shape, pieces, smallest, high):
    factor_of = 1.0
    for dim, parts in pieces:
        draws = jax.random.uniform(jax.random.fold_in(jax.random.fold_in(own_key, 6), dim), (parts,), jnp.float32, smallest / len(pieces), high / len(pieces))
        factor_of = factor_of * jnp.repeat(jnp.exp(draws), shape[dim] // parts).reshape((-1,) + (1,) * (len(shape) - 1 - dim))
    return factor_of


def scatter_about(stream_key, shape, scale, most, shards=(), kind=jnp.bfloat16):
    values = jax.random.normal(stream_key, shape, jnp.float32) * scale
    if len(shards) > 0:
        values = block_scale(stream_key, shape, shards, -0.22, 0.18) * values
    return jnp.clip(values, min=-most, max=most).astype(kind)


def setup_inputs(seed: int = 0) -> dict:
    seeds = jax.random.split(jax.random.key(seed), 5)
    grad_in = scatter_about(seeds[0], (SECTIONS, TOKENS, D), 1.0, 6.0, ((0, 16), (1, 16)))
    weights = scatter_about(seeds[1], (SECTIONS, D, D), D ** -0.5, 0.0625, ((0, 16), (1, 16)))
    band_index = place_ends(jax.random.randint(seeds[2], (SECTIONS, NB, 2), 0, D // BLK), jax.random.fold_in(seeds[2], 1), 0, (D // BLK) - 1).astype(jnp.int32)
    owner = jax.random.permutation(seeds[3], 2 * NB).astype(jnp.int32)
    return dict(grad_in=grad_in, weights=weights, band_index=band_index, owner=owner)


def section_pass(grad, weight):
    total = jnp.dot(grad, weight, preferred_element_type=jnp.float32)
    return (grad.astype(jnp.float32) + total).astype(jnp.bfloat16)


def gram_blocks(old, new, pairs):
    old_b = old.reshape(TOKENS, D // BLK, BLK).astype(jnp.float32)
    new_b = new.reshape(TOKENS, D // BLK, BLK).astype(jnp.float32)
    left = jnp.take(old_b, pairs[:, 0], axis=1)
    right_old = jnp.take(old_b, pairs[:, 1], axis=1)
    right_new = jnp.take(new_b, pairs[:, 1], axis=1)
    own = jnp.einsum('tkb,tkc->kbc', left, right_old)
    cross = jnp.einsum('tkb,tkc->kbc', left, right_new)
    return jnp.concatenate([own, cross], axis=0)


def reference(grad_in, weights, band_index, owner):
    grad = grad_in
    total = jnp.zeros((SECTIONS, 2 * NB, BLK, BLK), jnp.float32)

    def one_section(items):
        held, weight, pairs = items
        fresh = section_pass(held, weight)
        return fresh, gram_blocks(held, fresh, pairs)

    for step in range(STEPS):
        fresh, blocks = lax.map(one_section, (grad, weights, band_index))
        total = total + blocks
        grad = jnp.roll(fresh, -1, axis=0)
    factors = jnp.take(total, owner, axis=1) / float(TOKENS * STEPS)
    return factors, grad
```

```python
import functools

import jax
import jax.numpy as jnp
from jax import lax
from jax.experimental import pallas as pl
from jax.experimental.pallas import tpu as pltpu
from jax.sharding import PartitionSpec as P

D = 8192
BLK = 512
HALF = 256
NB = 8
STEPS = 2
TOKENS = 128
DP = 16
CHIPS = 8
TOK = TOKENS // DP
ROWS = 2 * TOK
BANDS = D // BLK
CHUNKS = 4
PER = BANDS // CHUNKS
MESH = pl.DeviceIdType.MESH
F32 = jnp.float32
BF16 = jnp.bfloat16

ROUTES = (
    ((1, 2), (1, 0), 4, ()),
    ((1, 1), (0, 1), 5, ()),
    ((1, 3), (0, 3), 6, ()),
    ((0, 1), (0, 1), 0, ()),
    ((0, 3), (0, 3), 1, ()),
    ((0, 2), (0, 2), 2, (4,)),
    ((1, 0), (1, 0), 3, (5, 6)),
    ((0, 0), None, None, ()),
)
SLOTS = 7
FINAL = 4


def folded(rows):
    cut = rows.reshape(rows.shape[0] // TOK, TOK, BLK)
    return jnp.concatenate([cut[:, :, :HALF], cut[:, :, HALF:]], axis=1)


def unfolded(blocks):
    wide = blocks.astype(F32)
    flat = jnp.concatenate([wide[:, :TOK], wide[:, TOK:]], axis=2)
    return flat.reshape(blocks.shape[0] * TOK, BLK)


def kernel(
    g_ref, w_hbm, band_ref, owner_ref, factors_ref, gout_ref,
    w, gtok, banded, x0, x1_out, x1,
    sib_out0, sib_in0, own0, rs_out0, rs_in0,
    sib_out1, sib_in1, own1, rs_out1, rs_in1,
    n0_out, right0, g1tok, right1, gout_in,
    l0_out, r0_out, l1_out, r1_out, l0_in, r0_in, l1_in, r1_in,
    w_sem, a2a_send, a2a_recv, sib_send0, sib_recv0, sib_send1, sib_recv1,
    rs_send0, rs_recv0, rs_send1, rs_recv1, pass_send, pass_recv, go_send, go_recv,
):
    sec = lax.axis_index("section")
    me = lax.axis_index("dp")
    secs = lax.axis_size("section")
    core = me % 2
    y = (me // 2) % 4
    x = me // 8
    before = (sec + secs - 1) % secs
    after = (sec + 1) % secs

    def chip(dx, dy):
        return ((x + dx) % 2) * 4 + (y + dy) % 4

    def peer(r):
        return chip(r // 8, (r // 2) % 4) * 2 + (core + r) % 2

    def remote(src, dst, send, recv, device):
        return pltpu.make_async_remote_copy(
            src_ref=src, dst_ref=dst, send_sem=send, recv_sem=recv,
            device_id=device, device_id_type=MESH,
        )

    def w_copy(k):
        cols = pl.ds(pl.multiple_of(chip(*ROUTES[k][0]) * 2 * BLK, 2 * BLK), 2 * BLK)
        return pltpu.make_async_copy(w_hbm.at[:, cols], w.at[:, cols], w_sem.at[k])

    for k in range(CHIPS):
        w_copy(k).start()

    barrier = pltpu.get_barrier_semaphore()

    def greet(r, carry):
        pl.semaphore_signal(barrier, inc=1, device_id=(sec, peer(r)), device_id_type=MESH)
        return carry

    lax.fori_loop(1, DP, greet, 0)
    pl.semaphore_signal(barrier, inc=1, device_id=(before, me), device_id_type=MESH)
    pl.semaphore_signal(barrier, inc=1, device_id=(after, me), device_id_type=MESH)

    wide = g_ref[...].astype(F32)
    for b in range(BANDS):
        gtok[b] = folded(wide[:, b * BLK:(b + 1) * BLK])[0].astype(BF16)

    pl.semaphore_wait(barrier, DP + 1)

    def exchange(which, out, into, base=0):
        def copy(r):
            q = peer(r)
            return remote(out.at[q], into.at[base + me], a2a_send.at[which, r], a2a_recv.at[which, r], (sec, q))

        def start():
            def body(r, carry):
                copy(r).start()
                return carry
            lax.fori_loop(1, DP, body, 0)
            into[base + me] = out[me]

        def recv():
            def body(r, carry):
                copy(r).wait_recv()
                return carry
            lax.fori_loop(1, DP, body, 0)

        def sent():
            def body(r, carry):
                copy(r).wait_send()
                return carry
            lax.fori_loop(1, DP, body, 0)

        return start, recv, sent

    a_start, a_recv, a_sent = exchange(0, gtok, banded)
    n_start, n_recv, n_sent = exchange(1, n0_out, right0, BANDS)
    l0_start, l0_recv, l0_sent = exchange(2, l0_out, l0_in)
    r0_start, r0_recv, r0_sent = exchange(3, r0_out, r0_in)
    l1_start, l1_recv, l1_sent = exchange(4, l1_out, l1_in)
    r1_start, r1_recv, r1_sent = exchange(5, r1_out, r1_in)

    a_start()

    def select(out, source, column):
        def body(q, carry):
            slot = owner_ref[q]
            k = slot % NB
            index = band_ref[k, column]
            if column == 1:
                index = index + (slot // NB) * BANDS
            out[q] = source[index]
            return carry
        lax.fori_loop(0, DP, body, 0)

    select(l0_out, gtok, 0)
    right0[:BANDS] = gtok[...]

    a_recv()
    x0[...] = unfolded(banded[...]).astype(BF16)

    def sibling0(k):
        return remote(sib_out0.at[k], sib_in0.at[k], sib_send0.at[k], sib_recv0.at[k], (sec, chip(0, 0) * 2 + 1 - core))

    def rs0(k):
        _, to, slot, _ = ROUTES[k]
        return remote(rs_out0.at[k], rs_in0.at[slot], rs_send0.at[k], rs_recv0.at[slot], (sec, chip(*to) * 2 + core))

    def arrived0(slot):
        k = [r[2] for r in ROUTES].index(slot)
        rs0(k).wait_recv()
        return rs_in0[slot].astype(F32)

    def compute0(k):
        m = chip(*ROUTES[k][0])
        w_copy(k).wait()
        other = pl.ds(pl.multiple_of((m * 2 + 1 - core) * BLK, BLK), BLK)
        mine = pl.ds(pl.multiple_of((m * 2 + core) * BLK, BLK), BLK)
        sib_out0[k] = jnp.dot(x0[...], w[:, other], preferred_element_type=F32).astype(BF16)
        sibling0(k).start()
        own0[k] = jnp.dot(x0[...], w[:, mine], preferred_element_type=F32)

    def finish0(k):
        sibling0(k).wait_recv()
        total = own0[k] + sib_in0[k].astype(F32)
        for slot in ROUTES[k][3]:
            total = total + arrived0(slot)
        if k < CHIPS - 1:
            rs_out0[k] = total.astype(BF16)
            rs0(k).start()
        else:
            own0[k] = total

    for k in range(CHIPS):
        compute0(k)
        if k > 0:
            finish0(k - 1)
    finish0(CHIPS - 1)
    total = own0[CHIPS - 1] + x0[...].astype(F32)
    for slot in range(FINAL):
        total = total + arrived0(slot)

    by_core = total.reshape(CHIPS, 2, TOK, BLK)
    first = core == 0
    x1_out[:TOKENS // 2] = jnp.where(first, by_core[:, 1], by_core[:, 0]).reshape(TOKENS // 2, BLK).astype(BF16)
    x1_out[TOKENS // 2:] = jnp.where(first, by_core[:, 0], by_core[:, 1]).reshape(TOKENS // 2, BLK).astype(BF16)
    band_pass = remote(x1_out, x1, pass_send.at[0], pass_recv.at[0], (before, me))
    band_pass.start()
    n0_out[...] = folded(total).astype(BF16)
    n_start()
    l0_start()

    token_pass = remote(right0.at[pl.ds(BANDS, BANDS)], g1tok, pass_send.at[1], pass_recv.at[1], (before, me))
    n_recv()
    token_pass.start()
    select(r0_out, right0, 1)
    r0_start()

    def sibling1(j):
        return remote(sib_out1.at[j], sib_in1.at[j], sib_send1.at[j], sib_recv1.at[j], (sec, chip(0, 0) * 2 + 1 - core))

    def rs1(j, k):
        _, to, slot, _ = ROUTES[k]
        return remote(rs_out1.at[j, k], rs_in1.at[j, slot], rs_send1.at[j, k], rs_recv1.at[j, slot], (sec, chip(*to) * 2 + core))

    def arrived1(j, slot):
        k = [r[2] for r in ROUTES].index(slot)
        rs1(j, k).wait_recv()
        return rs_in1[j, slot].astype(F32)

    def compute1(j):
        for e in range(PER):
            band = j * PER + e
            part = jnp.dot(x1[...], w[:, band * BLK:(band + 1) * BLK], preferred_element_type=F32)
            sib_out1[j, :, e] = folded(part[:TOKENS // 2]).astype(BF16)
            own1[j, :, e] = folded(part[TOKENS // 2:])
        sibling1(j).start()

    def finish1(j, ks):
        for k in ks:
            m = chip(*ROUTES[k][0])
            total = own1[j, m] + sib_in1[j, m].astype(F32)
            for slot in ROUTES[k][3]:
                total = total + arrived1(j, slot)
            rs_out1[j, k] = total.astype(BF16)
            rs1(j, k).start()

    def early1(j):
        sibling1(j).wait_recv()
        finish1(j, (0, 1, 2, 3, 4))

    def late1(j):
        finish1(j, (5, 6))

    def gout_copy(j):
        return remote(
            right1.at[pl.ds(BANDS + j * PER, PER)], gout_in.at[pl.ds(j * PER, PER)],
            go_send.at[j], go_recv.at[j], (before, me),
        )

    def last1(j):
        total = own1[j, chip(0, 0)] + sib_in1[j, chip(0, 0)].astype(F32)
        total = total + g1tok[j * PER:(j + 1) * PER].astype(F32)
        for slot in range(FINAL):
            total = total + arrived1(j, slot)
        right1[BANDS + j * PER:BANDS + (j + 1) * PER] = total.astype(BF16)
        gout_copy(j).start()

    band_pass.wait_recv()
    compute1(0)
    compute1(1)
    early1(0)
    compute1(2)
    early1(1)
    late1(0)
    compute1(3)
    early1(2)
    late1(1)
    early1(3)
    late1(2)
    late1(3)
    token_pass.wait_recv()
    select(l1_out, g1tok, 0)
    l1_start()
    right1[:BANDS] = g1tok[...]
    for j in range(CHUNKS):
        last1(j)
    select(r1_out, right1, 1)
    r1_start()

    def gram(left, right):
        return lax.dot_general(
            unfolded(left[...]).astype(BF16), unfolded(right[...]).astype(BF16),
            (((0,), (0,)), ((), ())), preferred_element_type=F32,
        )

    l0_recv()
    r0_recv()
    factors_ref[...] = gram(l0_in, r0_in)
    for j in range(CHUNKS):
        gout_copy(j).wait_recv()
    for b in range(BANDS):
        gout_ref[:, b * BLK:(b + 1) * BLK] = unfolded(gout_in[b:b + 1]).astype(BF16)
    l1_recv()
    r1_recv()
    factors_ref[...] = (factors_ref[...] + gram(l1_in, r1_in)) * (1.0 / (TOKENS * STEPS))

    a_sent()
    n_sent()
    l0_sent()
    r0_sent()
    l1_sent()
    r1_sent()
    band_pass.wait_send()
    token_pass.wait_send()
    for k in range(CHIPS):
        sibling0(k).wait_send()
        if k < CHIPS - 1:
            rs0(k).wait_send()
    for j in range(CHUNKS):
        sibling1(j).wait_send()
        gout_copy(j).wait_send()
        for k in range(CHIPS - 1):
            rs1(j, k).wait_send()


def shards(grad_in, weights, band_index, owner):
    vmem = pl.BlockSpec(memory_space=pltpu.VMEM)
    smem = pl.BlockSpec(memory_space=pltpu.SMEM)
    tok = (BANDS, ROWS, HALF)
    dma = pltpu.SemaphoreType.DMA
    factors, gout = pl.pallas_call(
        kernel,
        out_shape=(
            jax.ShapeDtypeStruct((BLK, BLK), F32),
            jax.ShapeDtypeStruct((TOK, D), BF16),
        ),
        in_specs=[vmem, pl.BlockSpec(memory_space=pl.ANY), smem, smem],
        out_specs=(vmem, vmem),
        scratch_shapes=[
            pltpu.VMEM((BLK, D), BF16),
            pltpu.VMEM(tok, BF16),
            pltpu.VMEM(tok, BF16),
            pltpu.VMEM((TOKENS, BLK), BF16),
            pltpu.VMEM((TOKENS, BLK), BF16),
            pltpu.VMEM((TOKENS, BLK), BF16),
            pltpu.VMEM((CHIPS, TOKENS, BLK), BF16),
            pltpu.VMEM((CHIPS, TOKENS, BLK), BF16),
            pltpu.VMEM((CHIPS, TOKENS, BLK), F32),
            pltpu.VMEM((SLOTS, TOKENS, BLK), BF16),
            pltpu.VMEM((SLOTS, TOKENS, BLK), BF16),
            pltpu.VMEM((CHUNKS, CHIPS, PER, ROWS, HALF), BF16),
            pltpu.VMEM((CHUNKS, CHIPS, PER, ROWS, HALF), BF16),
            pltpu.VMEM((CHUNKS, CHIPS, PER, ROWS, HALF), F32),
            pltpu.VMEM((CHUNKS, SLOTS, PER, ROWS, HALF), BF16),
            pltpu.VMEM((CHUNKS, SLOTS, PER, ROWS, HALF), BF16),
            pltpu.VMEM(tok, BF16),
            pltpu.VMEM((2 * BANDS, ROWS, HALF), BF16),
            pltpu.VMEM(tok, BF16),
            pltpu.VMEM((2 * BANDS, ROWS, HALF), BF16),
            pltpu.VMEM(tok, BF16),
        ] + [pltpu.VMEM(tok, BF16)] * 8 + [
            dma((CHIPS,)),
            dma((6, DP)),
            dma((6, DP)),
            dma((CHIPS,)),
            dma((CHIPS,)),
            dma((CHUNKS,)),
            dma((CHUNKS,)),
            dma((SLOTS,)),
            dma((SLOTS,)),
            dma((CHUNKS, SLOTS)),
            dma((CHUNKS, SLOTS)),
            dma((2,)),
            dma((2,)),
            dma((CHUNKS,)),
            dma((CHUNKS,)),
        ],
        compiler_params=pltpu.CompilerParams(
            collective_id=0, has_side_effects=True, vmem_limit_bytes=40 * 2 ** 20,
        ),
        name="relay",
    )(grad_in[0], weights[0], band_index[0], owner)
    return factors[None, None], gout[None]


def solution(mesh):
    return jax.shard_map(
        shards,
        mesh=mesh,
        in_specs=(
            P("section", "dp", None),
            P("section", "dp", None),
            P("section", None, None),
            P(),
        ),
        out_specs=(P("section", "dp", None, None), P("section", "dp", None)),
        check_vma=False,
    )
```

```python
import functools

import jax
import jax.numpy as jnp
from jax import lax
from jax.experimental import pallas as pl
from jax.experimental.pallas import tpu as pltpu
from jax.sharding import PartitionSpec as P

D = 8192
BLK = 512
HALF = 256
NB = 8
STEPS = 2
TOKENS = 128
DP = 16
CHIPS = 8
TOK = TOKENS // DP
ROWS = 2 * TOK
BANDS = D // BLK
CHUNKS = 4
PER = BANDS // CHUNKS
MESH = pl.DeviceIdType.MESH
F32 = jnp.float32
BF16 = jnp.bfloat16

ROUTES = (
    ((1, 1), (0, 1), 5, ()),
    ((1, 3), (0, 3), 6, ()),
    ((1, 2), (1, 0), 4, ()),
    ((0, 1), (0, 1), 0, ()),
    ((0, 3), (0, 3), 1, ()),
    ((0, 2), (0, 2), 2, (4,)),
    ((1, 0), (1, 0), 3, (5, 6)),
    ((0, 0), None, None, ()),
)
SLOTS = 7
PEERS = tuple(
    (dx, dy, dc)
    for dx, dy in ((1, 2), (1, 1), (1, 3), (0, 2), (1, 0), (0, 1), (0, 3), (0, 0))
    for dc in ((1, 0) if (dx, dy) != (0, 0) else (1,))
)
FINAL = 4


def folded(rows):
    cut = rows.reshape(rows.shape[0] // TOK, TOK, BLK)
    return jnp.concatenate([cut[:, :, :HALF], cut[:, :, HALF:]], axis=1)


def unfolded(blocks):
    wide = blocks.astype(F32)
    flat = jnp.concatenate([wide[:, :TOK], wide[:, TOK:]], axis=2)
    return flat.reshape(blocks.shape[0] * TOK, BLK)


def kernel(
    g_hbm, w_hbm, band_hbm, owner_hbm, factors_ref, gout_ref,
    g_ref, band_ref, owner_ref, w, gtok, banded, x0, x1_out, x1,
    sib_out0, sib_in0, own0, rs_out0, rs_in0,
    sib_out1, sib_in1, own1, rs_out1, rs_in1,
    n0_out, right0, g1tok, right1, gout_in,
    l0_out, r0_out, l1_out, r1_out, l0_in, r0_in, l1_in, r1_in,
    in_sem, w_sem, a2a_send, a2a_recv, sib_send0, sib_recv0, sib_send1, sib_recv1,
    rs_send0, rs_recv0, rs_send1, rs_recv1, pass_send, pass_recv, go_send, go_recv,
):
    sec = lax.axis_index("section")
    me = lax.axis_index("dp")
    secs = lax.axis_size("section")
    core = me % 2
    y = (me // 2) % 4
    x = me // 8
    before = (sec + secs - 1) % secs
    after = (sec + 1) % secs

    xs = (x, 1 - x)
    ys = tuple((y + d) % 4 for d in range(4))
    chips = {(dx, dy): xs[dx] * 4 + ys[dy] for dx in range(2) for dy in range(4)}

    def chip(dx, dy):
        return chips[dx, dy]

    def peer(r):
        dx, dy, dc = PEERS[r]
        return chips[dx, dy] * 2 + (core if dc == 0 else 1 - core)

    def remote(src, dst, send, recv, device):
        return pltpu.make_async_remote_copy(
            src_ref=src, dst_ref=dst, send_sem=send, recv_sem=recv,
            device_id=device, device_id_type=MESH,
        )

    def w_copy(k):
        cols = pl.ds(pl.multiple_of(chip(*ROUTES[k][0]) * 2 * BLK, 2 * BLK), 2 * BLK)
        return pltpu.make_async_copy(w_hbm.at[:, cols], w.at[:, cols], w_sem.at[k])

    barrier = pltpu.get_barrier_semaphore()
    for r in range(DP - 1):
        pl.semaphore_signal(barrier, inc=1, device_id=(sec, peer(r)), device_id_type=MESH)
    pl.semaphore_signal(barrier, inc=1, device_id=(before, me), device_id_type=MESH)
    pl.semaphore_signal(barrier, inc=1, device_id=(after, me), device_id_type=MESH)

    g_in = pltpu.make_async_copy(g_hbm, g_ref, in_sem.at[0])
    band_in = pltpu.make_async_copy(band_hbm, band_ref, in_sem.at[1])
    owner_in = pltpu.make_async_copy(owner_hbm, owner_ref, in_sem.at[2])
    g_in.start()
    band_in.start()
    owner_in.start()
    for k in range(CHIPS):
        w_copy(k).start()
    g_in.wait()
    wide = g_ref[...].astype(F32)
    for b in range(BANDS):
        gtok[b] = folded(wide[:, b * BLK:(b + 1) * BLK])[0].astype(BF16)

    pl.semaphore_wait(barrier, DP + 1)

    def exchange(which, out, into, base=0):
        def copy(r):
            q = peer(r)
            return remote(out.at[q], into.at[base + me], a2a_send.at[which, r], a2a_recv.at[which, r], (sec, q))

        def start():
            for r in range(DP - 1):
                copy(r).start()
            into[base + me] = out[me]

        def recv():
            for r in reversed(range(DP - 1)):
                copy(r).wait_recv()

        def sent():
            for r in range(DP - 1):
                copy(r).wait_send()

        return start, recv, sent

    a_start, a_recv, a_sent = exchange(0, gtok, banded)
    n_start, n_recv, n_sent = exchange(1, n0_out, right0, BANDS)
    l0_start, l0_recv, l0_sent = exchange(2, l0_out, l0_in)
    r0_start, r0_recv, r0_sent = exchange(3, r0_out, r0_in)
    l1_start, l1_recv, l1_sent = exchange(4, l1_out, l1_in)
    r1_start, r1_recv, r1_sent = exchange(5, r1_out, r1_in)

    a_start()
    band_in.wait()
    owner_in.wait()

    def select(out, source, column):
        for q in range(DP):
            slot = owner_ref[q]
            index = band_ref[column, slot % NB]
            if column == 1:
                index = index + (slot // NB) * BANDS
            out[q] = source[index]

    a_recv()
    x0[...] = unfolded(banded[...]).astype(BF16)

    def sibling0(k):
        return remote(sib_out0.at[k], sib_in0.at[k], sib_send0.at[k], sib_recv0.at[k], (sec, chip(0, 0) * 2 + 1 - core))

    def rs0(k):
        _, to, slot, _ = ROUTES[k]
        return remote(rs_out0.at[k], rs_in0.at[slot], rs_send0.at[k], rs_recv0.at[slot], (sec, chip(*to) * 2 + core))

    def arrived0(slot):
        k = [r[2] for r in ROUTES].index(slot)
        rs0(k).wait_recv()
        return rs_in0[slot].astype(F32)

    def other0(k):
        m = chip(*ROUTES[k][0])
        w_copy(k).wait()
        other = pl.ds(pl.multiple_of((m * 2 + 1 - core) * BLK, BLK), BLK)
        sib_out0[k] = jnp.dot(x0[...], w[:, other], preferred_element_type=F32).astype(BF16)
        sibling0(k).start()

    def mine0(k):
        m = chip(*ROUTES[k][0])
        mine = pl.ds(pl.multiple_of((m * 2 + core) * BLK, BLK), BLK)
        own0[k] = jnp.dot(x0[...], w[:, mine], preferred_element_type=F32)

    def finish0(k):
        sibling0(k).wait_recv()
        total = own0[k] + sib_in0[k].astype(F32)
        for slot in ROUTES[k][3]:
            total = total + arrived0(slot)
        if k < CHIPS - 1:
            rs_out0[k] = total.astype(BF16)
            rs0(k).start()
        else:
            own0[k] = total

    other0(0)
    for k in range(CHIPS):
        if k + 1 < CHIPS:
            other0(k + 1)
        mine0(k)
        finish0(k)
    total = own0[CHIPS - 1] + x0[...].astype(F32)
    for slot in range(FINAL):
        total = total + arrived0(slot)

    by_core = total.reshape(CHIPS, 2, TOK, BLK)
    first = core == 0
    x1_out[:TOKENS // 2] = jnp.where(first, by_core[:, 1], by_core[:, 0]).reshape(TOKENS // 2, BLK).astype(BF16)
    x1_out[TOKENS // 2:] = jnp.where(first, by_core[:, 0], by_core[:, 1]).reshape(TOKENS // 2, BLK).astype(BF16)
    band_pass = remote(x1_out, x1, pass_send.at[0], pass_recv.at[0], (before, me))
    band_pass.start()
    n0_out[...] = folded(total).astype(BF16)
    n_start()
    select(l0_out, gtok, 0)
    l0_start()
    right0[:BANDS] = gtok[...]

    token_pass = remote(right0.at[pl.ds(BANDS, BANDS)], g1tok, pass_send.at[1], pass_recv.at[1], (before, me))

    def sibling1(j):
        return remote(sib_out1.at[j], sib_in1.at[j], sib_send1.at[j], sib_recv1.at[j], (sec, chip(0, 0) * 2 + 1 - core))

    def rs1(j, k):
        _, to, slot, _ = ROUTES[k]
        return remote(rs_out1.at[j, k], rs_in1.at[j, slot], rs_send1.at[j, k], rs_recv1.at[j, slot], (sec, chip(*to) * 2 + core))

    def arrived1(j, slot):
        k = [r[2] for r in ROUTES].index(slot)
        rs1(j, k).wait_recv()
        return rs_in1[j, slot].astype(F32)

    def compute1(j):
        for e in range(PER):
            band = j * PER + e
            part = jnp.dot(x1[...], w[:, band * BLK:(band + 1) * BLK], preferred_element_type=F32)
            sib_out1[j, :, e] = folded(part[:TOKENS // 2]).astype(BF16)
            own1[j, :, e] = folded(part[TOKENS // 2:])
        sibling1(j).start()

    def finish1(j, ks):
        for k in ks:
            m = chip(*ROUTES[k][0])
            total = own1[j, m] + sib_in1[j, m].astype(F32)
            for slot in ROUTES[k][3]:
                total = total + arrived1(j, slot)
            rs_out1[j, k] = total.astype(BF16)
            rs1(j, k).start()

    def early1(j):
        sibling1(j).wait_recv()
        finish1(j, (0, 1, 2, 3, 4))

    def late1(j):
        finish1(j, (5, 6))

    def gout_copy(j):
        return remote(
            right1.at[pl.ds(BANDS + j * PER, PER)], gout_in.at[pl.ds(j * PER, PER)],
            go_send.at[j], go_recv.at[j], (before, me),
        )

    def last1(j):
        total = own1[j, chip(0, 0)] + sib_in1[j, chip(0, 0)].astype(F32)
        total = total + g1tok[j * PER:(j + 1) * PER].astype(F32)
        for slot in range(FINAL):
            total = total + arrived1(j, slot)
        right1[BANDS + j * PER:BANDS + (j + 1) * PER] = total.astype(BF16)
        gout_copy(j).start()

    band_pass.wait_recv()
    compute1(0)
    compute1(1)
    early1(0)
    n_recv()
    token_pass.start()
    compute1(2)
    early1(1)
    late1(0)
    select(r0_out, right0, 1)
    r0_start()
    compute1(3)
    early1(2)
    late1(1)
    early1(3)
    late1(2)
    late1(3)
    token_pass.wait_recv()
    select(l1_out, g1tok, 0)
    l1_start()
    right1[:BANDS] = g1tok[...]
    for j in range(CHUNKS):
        last1(j)
    select(r1_out, right1, 1)
    r1_start()

    def gram(left, right):
        return lax.dot_general(
            unfolded(left[...]).astype(BF16), unfolded(right[...]).astype(BF16),
            (((0,), (0,)), ((), ())), preferred_element_type=F32,
        )

    l0_recv()
    r0_recv()
    factors_ref[...] = gram(l0_in, r0_in)
    for j in range(CHUNKS):
        gout_copy(j).wait_recv()
    for b in range(BANDS):
        gout_ref[:, b * BLK:(b + 1) * BLK] = unfolded(gout_in[b:b + 1]).astype(BF16)
    l1_recv()
    r1_recv()
    factors_ref[...] = (factors_ref[...] + gram(l1_in, r1_in)) * (1.0 / (TOKENS * STEPS))

    a_sent()
    n_sent()
    l0_sent()
    r0_sent()
    l1_sent()
    r1_sent()
    band_pass.wait_send()
    token_pass.wait_send()
    for k in range(CHIPS):
        sibling0(k).wait_send()
        if k < CHIPS - 1:
            rs0(k).wait_send()
    for j in range(CHUNKS):
        sibling1(j).wait_send()
        gout_copy(j).wait_send()
        for k in range(CHIPS - 1):
            rs1(j, k).wait_send()


def shards(grad_in, weights, band_index, owner):
    vmem = pl.BlockSpec(memory_space=pltpu.VMEM)
    tok = (BANDS, ROWS, HALF)
    dma = pltpu.SemaphoreType.DMA
    factors, gout = pl.pallas_call(
        kernel,
        out_shape=(
            pltpu.VMEM((BLK, BLK), F32),
            pltpu.VMEM((TOK, D), BF16),
        ),
        in_specs=[pl.BlockSpec(memory_space=pl.ANY)] * 4,
        out_specs=(vmem, vmem),
        scratch_shapes=[
            pltpu.VMEM((TOK, D), BF16),
            pltpu.SMEM((2, NB), jnp.int32),
            pltpu.SMEM((DP,), jnp.int32),
            pltpu.VMEM((BLK, D), BF16),
            pltpu.VMEM(tok, BF16),
            pltpu.VMEM(tok, BF16),
            pltpu.VMEM((TOKENS, BLK), BF16),
            pltpu.VMEM((TOKENS, BLK), BF16),
            pltpu.VMEM((TOKENS, BLK), BF16),
            pltpu.VMEM((CHIPS, TOKENS, BLK), BF16),
            pltpu.VMEM((CHIPS, TOKENS, BLK), BF16),
            pltpu.VMEM((CHIPS, TOKENS, BLK), F32),
            pltpu.VMEM((SLOTS, TOKENS, BLK), BF16),
            pltpu.VMEM((SLOTS, TOKENS, BLK), BF16),
            pltpu.VMEM((CHUNKS, CHIPS, PER, ROWS, HALF), BF16),
            pltpu.VMEM((CHUNKS, CHIPS, PER, ROWS, HALF), BF16),
            pltpu.VMEM((CHUNKS, CHIPS, PER, ROWS, HALF), F32),
            pltpu.VMEM((CHUNKS, SLOTS, PER, ROWS, HALF), BF16),
            pltpu.VMEM((CHUNKS, SLOTS, PER, ROWS, HALF), BF16),
            pltpu.VMEM(tok, BF16),
            pltpu.VMEM((2 * BANDS, ROWS, HALF), BF16),
            pltpu.VMEM(tok, BF16),
            pltpu.VMEM((2 * BANDS, ROWS, HALF), BF16),
            pltpu.VMEM(tok, BF16),
        ] + [pltpu.VMEM(tok, BF16)] * 8 + [
            dma((3,)),
            dma((CHIPS,)),
            dma((6, DP)),
            dma((6, DP)),
            dma((CHIPS,)),
            dma((CHIPS,)),
            dma((CHUNKS,)),
            dma((CHUNKS,)),
            dma((SLOTS,)),
            dma((SLOTS,)),
            dma((CHUNKS, SLOTS)),
            dma((CHUNKS, SLOTS)),
            dma((2,)),
            dma((2,)),
            dma((CHUNKS,)),
            dma((CHUNKS,)),
        ],
        compiler_params=pltpu.CompilerParams(
            collective_id=0, has_side_effects=True, vmem_limit_bytes=58 * 2 ** 20,
        ),
        name="relay",
    )(grad_in[0], weights[0], band_index[0].T, owner)
    return factors[None, None], gout[None]


def solution(mesh):
    return jax.shard_map(
        shards,
        mesh=mesh,
        in_specs=(
            P("section", "dp", None),
            P("section", "dp", None),
            P("section", None, None),
            P(),
        ),
        out_specs=(P("section", "dp", None, None), P("section", "dp", None)),
        check_vma=False,
    )
```

```python
import functools

import jax
import jax.numpy as jnp
from jax import lax
from jax.experimental import pallas as pl
from jax.experimental.pallas import tpu as pltpu
from jax.sharding import PartitionSpec as P

D = 8192
BLK = 512
HALF = 256
NB = 8
STEPS = 2
TOKENS = 128
DP = 16
CHIPS = 8
TOK = TOKENS // DP
ROWS = 2 * TOK
BANDS = D // BLK
CORES = 2
ROWS0 = TOKENS // CORES
SIDE = BANDS // CORES
CHUNKS = 2
PER = SIDE // CHUNKS
MESH = pl.DeviceIdType.MESH
F32 = jnp.float32
BF16 = jnp.bfloat16

ROUTES = (
    ((1, 1), (0, 1), 5, ()),
    ((1, 3), (0, 3), 6, ()),
    ((1, 2), (1, 0), 4, ()),
    ((0, 1), (0, 1), 0, ()),
    ((0, 3), (0, 3), 1, ()),
    ((0, 2), (0, 2), 2, (4,)),
    ((1, 0), (1, 0), 3, (5, 6)),
    ((0, 0), None, None, ()),
)
SLOTS = 7
CHIP_ORDER = ((1, 2), (1, 1), (1, 3), (0, 2), (1, 0), (0, 1), (0, 3), (0, 0))
PEERS = tuple(r for r in range(DP) if r != DP - 2)
FINAL = 4
SENDER = tuple(next(k for k in range(SLOTS) if ROUTES[k][2] == slot) for slot in range(SLOTS))


def folded(rows):
    cut = rows.reshape(rows.shape[0] // TOK, TOK, BLK)
    return jnp.concatenate([cut[:, :, :HALF], cut[:, :, HALF:]], axis=1)


def unfolded(blocks):
    wide = blocks.astype(F32)
    flat = jnp.concatenate([wide[:, :TOK], wide[:, TOK:]], axis=2)
    return flat.reshape(blocks.shape[0] * TOK, BLK)


def kernel(
    g_hbm, w_hbm, band_hbm, owner_hbm, factors_ref, gout_ref,
    g_ref, band_ref, owner_ref, w, gtok, banded, x0, x1_out, x1,
    sib_out0, sib_in0, own0, rs_out0, rs_in0,
    sib_out1, sib_in1, own1, rs_out1, rs_in1,
    n0_out, right0, g1tok, own_out, own_in, fin, right1, gout_in,
    l0_out, rl_out, r1_out, l0_in, rl_in, r1_in,
    in_sem, w_sem, a2a_send, a2a_recv, sib_send0, sib_recv0, sib_send1, sib_recv1,
    rs_send0, rs_recv0, rs_send1, rs_recv1, fin_recv, pass_send, pass_recv, one_send, one_recv,
):
    sec = lax.axis_index("section")
    me = lax.axis_index("dp")
    secs = lax.axis_size("section")
    core = me % 2
    y = (me // 2) % 4
    x = me // 8
    before = (sec + secs - 1) % secs
    after = (sec + 1) % secs

    xs = (x, 1 - x)
    ys = tuple((y + d) % 4 for d in range(4))
    chips = {(dx, dy): xs[dx] * 4 + ys[dy] for dx in range(2) for dy in range(4)}

    def chip(dx, dy):
        return chips[dx, dy]

    here = chips[0, 0]
    sibling = here * 2 + 1 - core
    first = core == 0

    def peer(r):
        far = chips[CHIP_ORDER[r // 2]] * 2
        return far + (core if r % 2 == 0 else 1 - core)

    def remote(src, dst, send, recv, device):
        return pltpu.make_async_remote_copy(
            src_ref=src, dst_ref=dst, send_sem=send, recv_sem=recv,
            device_id=device, device_id_type=MESH,
        )

    def w_copy(k):
        cols = pl.ds(pl.multiple_of(chip(*ROUTES[k][0]) * 2 * BLK, 2 * BLK), 2 * BLK)
        return pltpu.make_async_copy(w_hbm.at[:, cols], w.at[:, cols], w_sem.at[k])

    barrier = pltpu.get_barrier_semaphore()
    for r in PEERS:
        pl.semaphore_signal(barrier, inc=1, device_id=(sec, peer(r)), device_id_type=MESH)
    for other_section in (before, after):
        pl.semaphore_signal(barrier, inc=1, device_id=(other_section, me), device_id_type=MESH)

    g_in = pltpu.make_async_copy(g_hbm, g_ref, in_sem.at[0])
    band_in = pltpu.make_async_copy(band_hbm, band_ref, in_sem.at[1])
    owner_in = pltpu.make_async_copy(owner_hbm, owner_ref, in_sem.at[2])
    g_in.start()
    band_in.start()
    owner_in.start()
    for k in range(CHIPS):
        w_copy(k).start()
    g_in.wait()
    wide = g_ref[...].astype(F32)
    for b in range(BANDS):
        gtok[b] = folded(wide[:, b * BLK:(b + 1) * BLK])[0].astype(BF16)

    pl.semaphore_wait(barrier, DP - 1 + 2)

    def all_of(ref, sem):
        pltpu.make_async_copy(ref, ref, sem).wait()

    def exchange(which, out, into):
        def start():
            for r in PEERS:
                q = peer(r)
                remote(out.at[q], into.at[me], a2a_send.at[which], a2a_recv.at[which], (sec, q)).start()
            into[me] = out[me]

        def recv():
            all_of(into.at[pl.ds(0, DP - 1)], a2a_recv.at[which])

        def sent():
            all_of(out.at[pl.ds(0, DP - 1)], a2a_send.at[which])

        return start, recv, sent

    a_start, a_recv, a_sent = exchange(0, gtok, banded)
    l0_start, l0_recv, l0_sent = exchange(2, l0_out, l0_in)
    rl_start, rl_recv, rl_sent = exchange(4, rl_out, rl_in)
    r1_start, r1_recv, r1_sent = exchange(5, r1_out, r1_in)

    a_start()
    band_in.wait()
    owner_in.wait()

    def select(out, source, column, part=None):
        for q in range(DP):
            slot = owner_ref[q]
            index = band_ref[column, slot % NB]
            if column == 1:
                index = index + (slot // NB) * BANDS
            if part is None:
                out[q] = source[index]
            else:
                out[q, part] = source[index]

    select(l0_out, gtok, 0)
    l0_start()
    a_recv()
    by_core = banded[...].reshape(CHIPS, CORES, ROWS, HALF)
    for h in range(CORES):
        x0[h] = unfolded(by_core[:, h]).astype(BF16)

    def to_sibling0(h, k):
        return remote(sib_out0.at[h, k], sib_in0.at[h, k], sib_send0, sib_recv0.at[h, k], (sec, sibling))

    def rs0(h, k):
        _, to, slot, _ = ROUTES[k]
        return remote(
            rs_out0.at[h, k], rs_in0.at[h, slot], rs_send0, rs_recv0.at[h, slot],
            (sec, chip(*to) * 2 + core),
        )

    def arrived0(h, slot):
        rs0(h, SENDER[slot]).wait_recv()
        return rs_in0[h, slot].astype(F32)

    def compute0(h, k):
        m = chip(*ROUTES[k][0])
        if h == 0:
            w_copy(k).wait()
        cols = pl.ds(pl.multiple_of(m * 2 * BLK, 2 * BLK), 2 * BLK)
        part = jnp.dot(x0[h], w[:, cols], preferred_element_type=F32)
        sib_out0[h, k] = jnp.where(first, part[:, BLK:], part[:, :BLK]).astype(BF16)
        to_sibling0(h, k).start()
        own0[h, k] = jnp.where(first, part[:, :BLK], part[:, BLK:])

    def finish0(h, k):
        to_sibling0(h, k).wait_recv()
        total = own0[h, k] + sib_in0[h, k].astype(F32)
        for slot in ROUTES[k][3]:
            total = total + arrived0(h, slot)
        rs_out0[h, k] = total.astype(BF16)
        rs0(h, k).start()

    def band_pass(h):
        return remote(x1_out.at[h], x1.at[h], pass_send.at[h], pass_recv.at[h], (before, me))

    def token_copy(h, c):
        to = chips[CHIP_ORDER[c]]
        return remote(
            n0_out.at[to, h], right0.at[BANDS + me], a2a_send.at[1], a2a_recv.at[1],
            (sec, to * 2 + h),
        )

    def last0(h):
        k = CHIPS - 1
        to_sibling0(h, k).wait_recv()
        total = own0[h, k] + sib_in0[h, k].astype(F32) + x0[h].astype(F32)
        for slot in range(FINAL):
            total = total + arrived0(h, slot)
        x1_out[h] = total.astype(BF16)
        band_pass(h).start()
        n0_out[:, h] = folded(total).astype(BF16)

    def spread(h):
        for c in range(CHIPS - 1):
            token_copy(h, c).start()

        @pl.when(core == h)
        def _():
            right0[BANDS + me] = n0_out[here, h]

        @pl.when(core != h)
        def _():
            token_copy(h, CHIPS - 1).start()

    token_pass = remote(right0.at[pl.ds(BANDS, BANDS)], g1tok, one_send.at[0], one_recv.at[0], (before, me))

    def tokens_on(h):
        @pl.when(core == h)
        def _():
            all_of(right0.at[pl.ds(BANDS, DP - 1)], a2a_recv.at[1])
            token_pass.start()

    def tokens_in(h):
        @pl.when(core == h)
        def _():
            token_pass.wait_recv()

    def to_sibling1(h, j):
        return remote(sib_out1.at[h, j], sib_in1.at[h, j], sib_send1, sib_recv1.at[h, j], (sec, sibling))

    def rs1(h, j, k):
        _, to, slot, _ = ROUTES[k]
        if slot < FINAL:
            return remote(rs_out1.at[h, j, k], fin.at[core, j, slot], rs_send1, fin_recv, (sec, chip(*to) * 2 + h))
        return remote(
            rs_out1.at[h, j, k], rs_in1.at[h, j, slot - FINAL], rs_send1, rs_recv1.at[h, j, slot - FINAL],
            (sec, chip(*to) * 2 + core),
        )

    def arrived1(h, j, slot):
        rs1(h, j, SENDER[slot]).wait_recv()
        return rs_in1[h, j, slot - FINAL].astype(F32)

    def to_owner(j):
        return remote(own_out.at[j], own_in.at[j], one_send.at[1], one_recv.at[1], (sec, sibling))

    def compute1(h, j):
        width = PER * BLK

        def part(c):
            cols = pl.ds(pl.multiple_of(c * SIDE * BLK + j * width, width), width)
            return jnp.dot(x1[h], w[:, cols], preferred_element_type=F32)

        other = part(1 - core)
        for e in range(PER):
            sib_out1[h, j, :, e] = folded(other[:, e * BLK:(e + 1) * BLK]).astype(BF16)
        to_sibling1(h, j).start()
        mine = part(core)
        for e in range(PER):
            own1[h, j, :, e] = folded(mine[:, e * BLK:(e + 1) * BLK])

    def finish1(h, j, ks):
        for k in ks:
            m = chip(*ROUTES[k][0])
            total = own1[h, j, m] + sib_in1[h, j, m].astype(F32)
            for slot in ROUTES[k][3]:
                total = total + arrived1(h, j, slot)
            rs_out1[h, j, k] = total.astype(BF16)
            rs1(h, j, k).start()

    def early1(h, j):
        to_sibling1(h, j).wait_recv()
        finish1(h, j, (0, 1, 2, 3, 4))

        @pl.when(core != h)
        def _():
            own_out[j] = (own1[h, j, here] + sib_in1[h, j, here].astype(F32)).astype(BF16)
            to_owner(j).start()

    def late1(h, j):
        finish1(h, j, (5, 6))

    gout_copy = remote(right1.at[pl.ds(BANDS, BANDS)], gout_in, one_send.at[2], one_recv.at[2], (before, me))

    def last1(h):
        @pl.when(core == h)
        def _():
            all_of(own_in, one_recv.at[1])
            all_of(fin, fin_recv)
            for p in range(CORES):
                for j in range(CHUNKS):
                    at = p * SIDE + j * PER
                    if p == h:
                        total = own1[h, j, here] + sib_in1[h, j, here].astype(F32)
                    else:
                        total = own_in[j].astype(F32)
                    total = total + g1tok[at:at + PER].astype(F32)
                    for slot in range(FINAL):
                        total = total + fin[p, j, slot].astype(F32)
                    right1[BANDS + at:BANDS + at + PER] = total.astype(BF16)
            gout_copy.start()
            select(r1_out, right1, 1)
            r1_start()

    compute0(0, 0)
    compute0(0, 1)
    compute0(0, 2)
    finish0(0, 0)
    compute0(0, 3)
    finish0(0, 1)
    compute0(0, 4)
    finish0(0, 2)
    compute0(0, 5)
    finish0(0, 3)
    compute0(0, 6)
    finish0(0, 4)
    compute0(0, 7)
    compute0(1, 0)
    finish0(0, 5)
    compute0(1, 1)
    finish0(0, 6)
    compute0(1, 2)
    finish0(1, 0)
    compute0(1, 3)
    finish0(1, 1)
    compute0(1, 4)
    finish0(1, 2)
    compute0(1, 5)
    finish0(1, 3)
    compute0(1, 6)
    finish0(1, 4)
    compute0(1, 7)
    last0(0)
    finish0(1, 5)
    finish0(1, 6)
    spread(0)
    right0[:BANDS] = gtok[...]
    band_pass(0).wait_recv()
    compute1(0, 0)
    compute1(0, 1)
    early1(0, 0)
    last0(1)
    spread(1)
    early1(0, 1)
    late1(0, 0)
    tokens_on(0)
    late1(0, 1)
    band_pass(1).wait_recv()
    compute1(1, 0)
    compute1(1, 1)
    early1(1, 0)
    early1(1, 1)
    tokens_on(1)
    late1(1, 0)
    late1(1, 1)
    tokens_in(0)
    tokens_in(1)
    right1[:BANDS] = g1tok[...]
    last1(0)
    select(rl_out, right0, 1, 0)
    select(rl_out, g1tok, 0, 1)
    rl_start()
    last1(1)

    def gram(left, right):
        return lax.dot_general(
            unfolded(left).astype(BF16), unfolded(right).astype(BF16),
            (((0,), (0,)), ((), ())), preferred_element_type=F32,
        )

    l0_recv()
    rl_recv()
    factors_ref[...] = gram(l0_in[...], rl_in[:, 0])
    gout_copy.wait_recv()
    for b in range(BANDS):
        gout_ref[:, b * BLK:(b + 1) * BLK] = unfolded(gout_in[b:b + 1]).astype(BF16)
    r1_recv()
    factors_ref[...] = (factors_ref[...] + gram(rl_in[:, 1], r1_in[...])) * (1.0 / (TOKENS * STEPS))

    a_sent()
    l0_sent()
    rl_sent()
    r1_sent()
    token_pass.wait_send()
    gout_copy.wait_send()
    all_of(own_out, one_send.at[1])
    all_of(n0_out.at[:CHIPS - 1], a2a_send.at[1])
    all_of(n0_out.at[0, 0], a2a_send.at[1])
    for h in range(CORES):
        band_pass(h).wait_send()
    all_of(sib_out0, sib_send0)
    all_of(rs_out0, rs_send0)
    all_of(sib_out1, sib_send1)
    all_of(rs_out1, rs_send1)


def shards(grad_in, weights, band_index, owner):
    vmem = pl.BlockSpec(memory_space=pltpu.VMEM)
    tok = (BANDS, ROWS, HALF)
    dma = pltpu.SemaphoreType.DMA
    factors, gout = pl.pallas_call(
        kernel,
        out_shape=(
            pltpu.VMEM((BLK, BLK), F32),
            pltpu.VMEM((TOK, D), BF16),
        ),
        in_specs=[pl.BlockSpec(memory_space=pl.ANY)] * 4,
        out_specs=(vmem, vmem),
        scratch_shapes=[
            pltpu.VMEM((TOK, D), BF16),
            pltpu.SMEM((2, NB), jnp.int32),
            pltpu.SMEM((DP,), jnp.int32),
            pltpu.VMEM((BLK, D), BF16),
            pltpu.VMEM(tok, BF16),
            pltpu.VMEM(tok, BF16),
            pltpu.VMEM((CORES, ROWS0, BLK), BF16),
            pltpu.VMEM((CORES, ROWS0, BLK), BF16),
            pltpu.VMEM((CORES, ROWS0, BLK), BF16),
            pltpu.VMEM((CORES, CHIPS, ROWS0, BLK), BF16),
            pltpu.VMEM((CORES, CHIPS, ROWS0, BLK), BF16),
            pltpu.VMEM((CORES, CHIPS, ROWS0, BLK), F32),
            pltpu.VMEM((CORES, SLOTS, ROWS0, BLK), BF16),
            pltpu.VMEM((CORES, SLOTS, ROWS0, BLK), BF16),
            pltpu.VMEM((CORES, CHUNKS, CHIPS, PER, ROWS, HALF), BF16),
            pltpu.VMEM((CORES, CHUNKS, CHIPS, PER, ROWS, HALF), BF16),
            pltpu.VMEM((CORES, CHUNKS, CHIPS, PER, ROWS, HALF), F32),
            pltpu.VMEM((CORES, CHUNKS, SLOTS, PER, ROWS, HALF), BF16),
            pltpu.VMEM((CORES, CHUNKS, SLOTS - FINAL, PER, ROWS, HALF), BF16),
            pltpu.VMEM((CHIPS, CORES, ROWS, HALF), BF16),
            pltpu.VMEM((2 * BANDS, ROWS, HALF), BF16),
            pltpu.VMEM(tok, BF16),
            pltpu.VMEM((CHUNKS, PER, ROWS, HALF), BF16),
            pltpu.VMEM((CHUNKS, PER, ROWS, HALF), BF16),
            pltpu.VMEM((CORES, CHUNKS, FINAL, PER, ROWS, HALF), BF16),
            pltpu.VMEM((2 * BANDS, ROWS, HALF), BF16),
            pltpu.VMEM(tok, BF16),
            pltpu.VMEM(tok, BF16),
            pltpu.VMEM((DP, 2, ROWS, HALF), BF16),
            pltpu.VMEM(tok, BF16),
            pltpu.VMEM(tok, BF16),
            pltpu.VMEM((DP, 2, ROWS, HALF), BF16),
            pltpu.VMEM(tok, BF16),
            dma((3,)),
            dma((CHIPS,)),
            dma((6,)),
            dma((6,)),
            dma,
            dma((CORES, CHIPS)),
            dma,
            dma((CORES, CHUNKS)),
            dma,
            dma((CORES, SLOTS)),
            dma,
            dma((CORES, CHUNKS, SLOTS - FINAL)),
            dma,
            dma((CORES,)),
            dma((CORES,)),
            dma((3,)),
            dma((3,)),
        ],
        compiler_params=pltpu.CompilerParams(
            collective_id=0, has_side_effects=True, vmem_limit_bytes=58 * 2 ** 20,
        ),
        name="relay",
    )(grad_in[0], weights[0], band_index[0].T, owner)
    return factors[None, None], gout[None]


def solution(mesh):
    return jax.shard_map(
        shards,
        mesh=mesh,
        in_specs=(
            P("section", "dp", None),
            P("section", "dp", None),
            P("section", None, None),
            P(),
        ),
        out_specs=(P("section", "dp", None, None), P("section", "dp", None)),
        check_vma=False,
    )
```

```python
import functools

import jax
import jax.numpy as jnp
from jax import lax
from jax.experimental import pallas as pl
from jax.experimental.pallas import tpu as pltpu
from jax.sharding import PartitionSpec as P

D = 8192
BLK = 512
HALF = 256
NB = 8
STEPS = 2
TOKENS = 128
DP = 16
CHIPS = 8
TOK = TOKENS // DP
ROWS = 2 * TOK
BANDS = D // BLK
CORES = 2
ROWS0 = TOKENS // CORES
SIDE = BANDS // CORES
CHUNKS = 1
PER = SIDE // CHUNKS
MESH = pl.DeviceIdType.MESH
F32 = jnp.float32
BF16 = jnp.bfloat16

ROUTES = (
    ((1, 2), (1, 0), 4, ()),
    ((1, 1), (0, 1), 5, ()),
    ((1, 3), (0, 3), 6, ()),
    ((0, 1), (0, 1), 0, ()),
    ((0, 3), (0, 3), 1, ()),
    ((0, 2), (0, 2), 2, (4,)),
    ((1, 0), (1, 0), 3, (5, 6)),
    ((0, 0), None, None, ()),
)
SLOTS = 7
CHIP_ORDER = ((1, 2), (1, 1), (1, 3), (0, 2), (1, 0), (0, 1), (0, 3), (0, 0))
PEERS = tuple(r for r in range(DP) if r != DP - 2)
FINAL = 4
SENDER = tuple(next(k for k in range(SLOTS) if ROUTES[k][2] == slot) for slot in range(SLOTS))


def folded(rows):
    cut = rows.reshape(rows.shape[0] // TOK, TOK, BLK)
    return jnp.concatenate([cut[:, :, :HALF], cut[:, :, HALF:]], axis=1)


def unfolded(blocks):
    wide = blocks.astype(F32)
    flat = jnp.concatenate([wide[:, :TOK], wide[:, TOK:]], axis=2)
    return flat.reshape(blocks.shape[0] * TOK, BLK)


def kernel(
    g_hbm, w_hbm, band_hbm, owner_hbm, factors_ref, gout_ref,
    g_ref, band_ref, owner_ref, w, gtok, banded, x0, x1_out, x1,
    sib_out0, sib_in0, own0, rs_out0, rs_in0,
    sib_out1, sib_in1, own1, rs_out1, rs_in1,
    n0_out, right0, g1tok, own_out, own_in, fin, right1, gout_in,
    l0_out, rl_out, r1_out, l0_in, rl_in, r1_in,
    in_sem, w_sem, a2a_send, a2a_recv, sib_send0, sib_recv0, sib_send1, sib_recv1,
    rs_send0, rs_recv0, rs_send1, rs_recv1, fin_recv, pass_send, pass_recv, one_send, one_recv,
):
    sec = lax.axis_index("section")
    me = lax.axis_index("dp")
    secs = lax.axis_size("section")
    core = me % 2
    y = (me // 2) % 4
    x = me // 8
    before = (sec + secs - 1) % secs
    after = (sec + 1) % secs

    xs = (x, 1 - x)
    ys = tuple((y + d) % 4 for d in range(4))
    chips = {(dx, dy): xs[dx] * 4 + ys[dy] for dx in range(2) for dy in range(4)}

    def chip(dx, dy):
        return chips[dx, dy]

    here = chips[0, 0]
    sibling = here * 2 + 1 - core
    first = core == 0

    def peer(r):
        far = chips[CHIP_ORDER[r // 2]] * 2
        return far + (core if r % 2 == 0 else 1 - core)

    def remote(src, dst, send, recv, device):
        return pltpu.make_async_remote_copy(
            src_ref=src, dst_ref=dst, send_sem=send, recv_sem=recv,
            device_id=device, device_id_type=MESH,
        )

    def w_copy(k):
        cols = pl.ds(pl.multiple_of(chip(*ROUTES[k][0]) * 2 * BLK, 2 * BLK), 2 * BLK)
        return pltpu.make_async_copy(w_hbm.at[:, cols], w.at[:, cols], w_sem.at[k])

    barrier = pltpu.get_barrier_semaphore()
    for r in PEERS:
        pl.semaphore_signal(barrier, inc=1, device_id=(sec, peer(r)), device_id_type=MESH)
    for other_section in (before, after):
        pl.semaphore_signal(barrier, inc=1, device_id=(other_section, me), device_id_type=MESH)

    g_in = pltpu.make_async_copy(g_hbm, g_ref, in_sem.at[0])
    band_in = pltpu.make_async_copy(band_hbm, band_ref, in_sem.at[1])
    owner_in = pltpu.make_async_copy(owner_hbm, owner_ref, in_sem.at[2])
    g_in.start()
    band_in.start()
    owner_in.start()
    for k in range(CHIPS):
        w_copy(k).start()
    g_in.wait()
    wide = g_ref[...].astype(F32)
    for b in range(BANDS):
        gtok[b] = folded(wide[:, b * BLK:(b + 1) * BLK])[0].astype(BF16)

    pl.semaphore_wait(barrier, DP - 1 + 2)

    def all_of(ref, sem):
        pltpu.make_async_copy(ref, ref, sem).wait()

    def exchange(which, out, into):
        def start():
            for r in PEERS:
                q = peer(r)
                remote(out.at[q], into.at[me], a2a_send.at[which], a2a_recv.at[which], (sec, q)).start()
            into[me] = out[me]

        def recv():
            all_of(into.at[pl.ds(0, DP - 1)], a2a_recv.at[which])

        def sent():
            all_of(out.at[pl.ds(0, DP - 1)], a2a_send.at[which])

        return start, recv, sent

    a_start, a_recv, a_sent = exchange(0, gtok, banded)
    l0_start, l0_recv, l0_sent = exchange(2, l0_out, l0_in)
    rl_start, rl_recv, rl_sent = exchange(4, rl_out, rl_in)
    r1_start, r1_recv, r1_sent = exchange(5, r1_out, r1_in)

    a_start()
    band_in.wait()
    owner_in.wait()

    def select(out, source, column, part=None):
        for q in range(DP):
            slot = owner_ref[q]
            index = band_ref[column, slot % NB]
            if column == 1:
                index = index + (slot // NB) * BANDS
            if part is None:
                out[q] = source[index]
            else:
                out[q, part] = source[index]

    select(l0_out, gtok, 0)
    l0_start()
    a_recv()
    by_core = banded[...].reshape(CHIPS, CORES, ROWS, HALF)
    for h in range(CORES):
        x0[h] = unfolded(by_core[:, h]).astype(BF16)

    def to_sibling0(h, n):
        pair = pl.ds(2 * n, 2)
        return remote(
            sib_out0.at[h, pair], sib_in0.at[h, pair], sib_send0, sib_recv0.at[h, n], (sec, sibling),
        )

    shared = set()

    def shared0(h, k):
        if (h, k // 2) not in shared:
            shared.add((h, k // 2))
            to_sibling0(h, k // 2).wait_recv()

    def rs0(h, k):
        _, to, slot, _ = ROUTES[k]
        return remote(
            rs_out0.at[h, k], rs_in0.at[h, slot], rs_send0, rs_recv0.at[h, slot],
            (sec, chip(*to) * 2 + core),
        )

    def arrived0(h, slot):
        rs0(h, SENDER[slot]).wait_recv()
        return rs_in0[h, slot].astype(F32)

    def compute0(h, n):
        for k in (2 * n, 2 * n + 1):
            if h == 0:
                w_copy(k).wait()
        for k in (2 * n, 2 * n + 1):
            cols = pl.ds(pl.multiple_of(chip(*ROUTES[k][0]) * 2 * BLK, 2 * BLK), 2 * BLK)
            part = jnp.dot(x0[h], w[:, cols], preferred_element_type=F32)
            sib_out0[h, k] = jnp.where(first, part[:, BLK:], part[:, :BLK]).astype(BF16)
            own0[h, k] = jnp.where(first, part[:, :BLK], part[:, BLK:])
        to_sibling0(h, n).start()

    def finish0(h, *ks):
        for k in ks:
            shared0(h, k)
            for slot in ROUTES[k][3]:
                rs0(h, SENDER[slot]).wait_recv()
        for k in ks:
            total = own0[h, k] + sib_in0[h, k].astype(F32)
            for slot in ROUTES[k][3]:
                total = total + rs_in0[h, slot].astype(F32)
            rs_out0[h, k] = total.astype(BF16)
        for k in ks:
            rs0(h, k).start()

    def band_pass(h):
        return remote(x1_out.at[h], x1.at[h], pass_send.at[h], pass_recv.at[h], (before, me))

    def token_copy(h, c):
        to = chips[CHIP_ORDER[c]]
        return remote(
            n0_out.at[to, h], right0.at[BANDS + me], a2a_send.at[1], a2a_recv.at[1],
            (sec, to * 2 + h),
        )

    def last0(h):
        k = CHIPS - 1
        shared0(h, k)
        total = own0[h, k] + sib_in0[h, k].astype(F32) + x0[h].astype(F32)
        for slot in range(FINAL):
            total = total + arrived0(h, slot)
        x1_out[h] = total.astype(BF16)
        band_pass(h).start()
        n0_out[:, h] = folded(total).astype(BF16)

    def spread(h):
        for c in range(CHIPS - 1):
            token_copy(h, c).start()

        @pl.when(core == h)
        def _():
            right0[BANDS + me] = n0_out[here, h]

        @pl.when(core != h)
        def _():
            token_copy(h, CHIPS - 1).start()

    token_pass = remote(right0.at[pl.ds(BANDS, BANDS)], g1tok, one_send.at[0], one_recv.at[0], (before, me))

    def tokens_on(h):
        @pl.when(core == h)
        def _():
            all_of(right0.at[pl.ds(BANDS, DP - 1)], a2a_recv.at[1])
            token_pass.start()

    def tokens_in(h):
        @pl.when(core == h)
        def _():
            token_pass.wait_recv()

    def to_sibling1(h, j):
        return remote(sib_out1.at[h, j], sib_in1.at[h, j], sib_send1, sib_recv1.at[h, j], (sec, sibling))

    def rs1(h, j, k):
        _, to, slot, _ = ROUTES[k]
        if slot < FINAL:
            return remote(rs_out1.at[h, j, k], fin.at[core, j, slot], rs_send1, fin_recv, (sec, chip(*to) * 2 + h))
        return remote(
            rs_out1.at[h, j, k], rs_in1.at[h, j, slot - FINAL], rs_send1, rs_recv1.at[h, j, slot - FINAL],
            (sec, chip(*to) * 2 + core),
        )

    def arrived1(h, j, slot):
        rs1(h, j, SENDER[slot]).wait_recv()
        return rs_in1[h, j, slot - FINAL].astype(F32)

    def to_owner(j):
        return remote(own_out.at[j], own_in.at[j], one_send.at[1], one_recv.at[1], (sec, sibling))

    def compute1(h, j):
        width = PER * BLK

        def part(c):
            cols = pl.ds(pl.multiple_of(c * SIDE * BLK + j * width, width), width)
            return jnp.dot(x1[h], w[:, cols], preferred_element_type=F32)

        other = part(1 - core)
        for e in range(PER):
            sib_out1[h, j, :, e] = folded(other[:, e * BLK:(e + 1) * BLK]).astype(BF16)
        to_sibling1(h, j).start()
        mine = part(core)
        for e in range(PER):
            own1[h, j, :, e] = folded(mine[:, e * BLK:(e + 1) * BLK])

    def finish1(h, j, ks):
        for k in ks:
            m = chip(*ROUTES[k][0])
            total = own1[h, j, m] + sib_in1[h, j, m].astype(F32)
            for slot in ROUTES[k][3]:
                total = total + arrived1(h, j, slot)
            rs_out1[h, j, k] = total.astype(BF16)
            rs1(h, j, k).start()

    def early1(h, j):
        to_sibling1(h, j).wait_recv()
        finish1(h, j, (0, 1, 2, 3, 4))

        @pl.when(core != h)
        def _():
            own_out[j] = (own1[h, j, here] + sib_in1[h, j, here].astype(F32)).astype(BF16)
            to_owner(j).start()

    def late1(h, j):
        finish1(h, j, (5, 6))

    gout_copy = remote(right1.at[pl.ds(BANDS, BANDS)], gout_in, one_send.at[2], one_recv.at[2], (before, me))

    def last1(h):
        @pl.when(core == h)
        def _():
            all_of(own_in, one_recv.at[1])
            all_of(fin, fin_recv)
            for p in range(CORES):
                for j in range(CHUNKS):
                    at = p * SIDE + j * PER
                    if p == h:
                        total = own1[h, j, here] + sib_in1[h, j, here].astype(F32)
                    else:
                        total = own_in[j].astype(F32)
                    total = total + g1tok[at:at + PER].astype(F32)
                    for slot in range(FINAL):
                        total = total + fin[p, j, slot].astype(F32)
                    right1[BANDS + at:BANDS + at + PER] = total.astype(BF16)
            gout_copy.start()
            select(r1_out, right1, 1)
            r1_start()

    compute0(0, 0)
    compute0(0, 1)
    finish0(0, 0, 1)
    compute0(0, 2)
    finish0(0, 2, 3)
    compute0(0, 3)
    finish0(0, 4)
    compute0(1, 0)
    finish0(0, 5)
    finish0(0, 6)
    compute0(1, 1)
    finish0(1, 0, 1)
    compute0(1, 2)
    finish0(1, 2, 3)
    compute0(1, 3)
    finish0(1, 4)
    last0(0)
    finish0(1, 5)
    finish0(1, 6)
    spread(0)
    right0[:BANDS] = gtok[...]
    band_pass(0).wait_recv()
    compute1(0, 0)
    early1(0, 0)
    last0(1)
    spread(1)
    late1(0, 0)
    tokens_on(0)
    band_pass(1).wait_recv()
    compute1(1, 0)
    early1(1, 0)
    tokens_on(1)
    late1(1, 0)
    tokens_in(0)
    tokens_in(1)
    right1[:BANDS] = g1tok[...]
    last1(0)
    select(rl_out, right0, 1, 0)
    select(rl_out, g1tok, 0, 1)
    rl_start()
    last1(1)

    def gram(left, right):
        return lax.dot_general(
            unfolded(left).astype(BF16), unfolded(right).astype(BF16),
            (((0,), (0,)), ((), ())), preferred_element_type=F32,
        )

    l0_recv()
    rl_recv()
    factors_ref[...] = gram(l0_in[...], rl_in[:, 0])
    gout_copy.wait_recv()
    for b in range(BANDS):
        gout_ref[:, b * BLK:(b + 1) * BLK] = unfolded(gout_in[b:b + 1]).astype(BF16)
    a_sent()
    l0_sent()
    rl_sent()
    token_pass.wait_send()
    gout_copy.wait_send()
    all_of(own_out, one_send.at[1])
    all_of(n0_out.at[:CHIPS - 1], a2a_send.at[1])
    all_of(n0_out.at[0, 0], a2a_send.at[1])
    for h in range(CORES):
        band_pass(h).wait_send()
    all_of(sib_out0, sib_send0)
    all_of(rs_out0, rs_send0)
    all_of(sib_out1, sib_send1)
    all_of(rs_out1, rs_send1)
    r1_recv()
    factors_ref[...] = (factors_ref[...] + gram(rl_in[:, 1], r1_in[...])) * (1.0 / (TOKENS * STEPS))

    r1_sent()


def shards(grad_in, weights, band_index, owner):
    vmem = pl.BlockSpec(memory_space=pltpu.VMEM)
    tok = (BANDS, ROWS, HALF)
    dma = pltpu.SemaphoreType.DMA
    factors, gout = pl.pallas_call(
        kernel,
        out_shape=(
            pltpu.VMEM((BLK, BLK), F32),
            pltpu.VMEM((TOK, D), BF16),
        ),
        in_specs=[pl.BlockSpec(memory_space=pl.ANY)] * 4,
        out_specs=(vmem, vmem),
        scratch_shapes=[
            pltpu.VMEM((TOK, D), BF16),
            pltpu.SMEM((2, NB), jnp.int32),
            pltpu.SMEM((DP,), jnp.int32),
            pltpu.VMEM((BLK, D), BF16),
            pltpu.VMEM(tok, BF16),
            pltpu.VMEM(tok, BF16),
            pltpu.VMEM((CORES, ROWS0, BLK), BF16),
            pltpu.VMEM((CORES, ROWS0, BLK), BF16),
            pltpu.VMEM((CORES, ROWS0, BLK), BF16),
            pltpu.VMEM((CORES, CHIPS, ROWS0, BLK), BF16),
            pltpu.VMEM((CORES, CHIPS, ROWS0, BLK), BF16),
            pltpu.VMEM((CORES, CHIPS, ROWS0, BLK), F32),
            pltpu.VMEM((CORES, SLOTS, ROWS0, BLK), BF16),
            pltpu.VMEM((CORES, SLOTS, ROWS0, BLK), BF16),
            pltpu.VMEM((CORES, CHUNKS, CHIPS, PER, ROWS, HALF), BF16),
            pltpu.VMEM((CORES, CHUNKS, CHIPS, PER, ROWS, HALF), BF16),
            pltpu.VMEM((CORES, CHUNKS, CHIPS, PER, ROWS, HALF), F32),
            pltpu.VMEM((CORES, CHUNKS, SLOTS, PER, ROWS, HALF), BF16),
            pltpu.VMEM((CORES, CHUNKS, SLOTS - FINAL, PER, ROWS, HALF), BF16),
            pltpu.VMEM((CHIPS, CORES, ROWS, HALF), BF16),
            pltpu.VMEM((2 * BANDS, ROWS, HALF), BF16),
            pltpu.VMEM(tok, BF16),
            pltpu.VMEM((CHUNKS, PER, ROWS, HALF), BF16),
            pltpu.VMEM((CHUNKS, PER, ROWS, HALF), BF16),
            pltpu.VMEM((CORES, CHUNKS, FINAL, PER, ROWS, HALF), BF16),
            pltpu.VMEM((2 * BANDS, ROWS, HALF), BF16),
            pltpu.VMEM(tok, BF16),
            pltpu.VMEM(tok, BF16),
            pltpu.VMEM((DP, 2, ROWS, HALF), BF16),
            pltpu.VMEM(tok, BF16),
            pltpu.VMEM(tok, BF16),
            pltpu.VMEM((DP, 2, ROWS, HALF), BF16),
            pltpu.VMEM(tok, BF16),
            dma((3,)),
            dma((CHIPS,)),
            dma((6,)),
            dma((6,)),
            dma,
            dma((CORES, CHIPS // 2)),
            dma,
            dma((CORES, CHUNKS)),
            dma,
            dma((CORES, SLOTS)),
            dma,
            dma((CORES, CHUNKS, SLOTS - FINAL)),
            dma,
            dma((CORES,)),
            dma((CORES,)),
            dma((3,)),
            dma((3,)),
        ],
        compiler_params=pltpu.CompilerParams(
            collective_id=0, has_side_effects=True, vmem_limit_bytes=58 * 2 ** 20,
        ),
        name="relay",
    )(grad_in[0], weights[0], band_index[0].T, owner)
    return factors[None, None], gout[None]


def solution(mesh):
    return jax.shard_map(
        shards,
        mesh=mesh,
        in_specs=(
            P("section", "dp", None),
            P("section", "dp", None),
            P("section", None, None),
            P(),
        ),
        out_specs=(P("section", "dp", None, None), P("section", "dp", None)),
        check_vma=False,
    )
```

```python
import functools

import jax
import jax.numpy as jnp
from jax import lax
from jax.experimental import pallas as pl
from jax.experimental.pallas import tpu as pltpu
from jax.sharding import PartitionSpec as P

D = 8192
BLK = 512
HALF = 256
NB = 8
STEPS = 2
TOKENS = 128
DP = 16
CHIPS = 8
TOK = TOKENS // DP
ROWS = 2 * TOK
BANDS = D // BLK
CORES = 2
ROWS0 = TOKENS // CORES
SIDE = BANDS // CORES
CHUNKS = 1
PER = SIDE // CHUNKS
MESH = pl.DeviceIdType.MESH
F32 = jnp.float32
BF16 = jnp.bfloat16

ROUTES = (
    ((1, 2), (1, 0), 4, ()),
    ((1, 1), (0, 1), 5, ()),
    ((1, 3), (0, 3), 6, ()),
    ((0, 1), (0, 1), 0, ()),
    ((0, 3), (0, 3), 1, ()),
    ((0, 2), (0, 2), 2, (4,)),
    ((1, 0), (1, 0), 3, (5, 6)),
    ((0, 0), None, None, ()),
)
SLOTS = 7
CHIP_ORDER = ((1, 2), (1, 1), (1, 3), (0, 2), (1, 0), (0, 1), (0, 3), (0, 0))
PEERS = tuple(r for r in range(DP) if r != DP - 2)
FINAL = 4
SENDER = tuple(next(k for k in range(SLOTS) if ROUTES[k][2] == slot) for slot in range(SLOTS))


def folded(rows):
    cut = rows.reshape(rows.shape[0] // TOK, TOK, BLK)
    return jnp.concatenate([cut[:, :, :HALF], cut[:, :, HALF:]], axis=1)


def unfolded(blocks):
    wide = blocks.astype(F32)
    flat = jnp.concatenate([wide[:, :TOK], wide[:, TOK:]], axis=2)
    return flat.reshape(blocks.shape[0] * TOK, BLK)


def kernel(
    g_hbm, w_hbm, band_hbm, owner_hbm, factors_ref, gout_ref,
    g_ref, band_ref, owner_ref, w, gtok, banded, x0, x1_out, x1,
    sib_out0, sib_in0, own0, rs_out0, rs_in0,
    sib_out1, sib_in1, own1, rs_out1, rs_in1,
    n0_out, right0, g1tok, own_out, own_in, fin, right1, gout_in,
    l0_out, r0_out, l1_out, r1_out, l0_in, r0_in, l1_in, r1_in,
    in_sem, w_sem, a2a_send, a2a_recv, sib_send0, sib_recv0, sib_send1, sib_recv1,
    rs_send0, rs_recv0, rs_send1, rs_recv1, fin_recv, pass_send, pass_recv, one_send, one_recv,
):
    sec = lax.axis_index("section")
    me = lax.axis_index("dp")
    secs = lax.axis_size("section")
    core = me % 2
    y = (me // 2) % 4
    x = me // 8
    before = (sec + secs - 1) % secs
    after = (sec + 1) % secs

    xs = (x, 1 - x)
    ys = tuple((y + d) % 4 for d in range(4))
    chips = {(dx, dy): xs[dx] * 4 + ys[dy] for dx in range(2) for dy in range(4)}

    def chip(dx, dy):
        return chips[dx, dy]

    here = chips[0, 0]
    sibling = here * 2 + 1 - core
    first = core == 0

    def peer(r):
        far = chips[CHIP_ORDER[r // 2]] * 2
        return far + (core if r % 2 == 0 else 1 - core)

    def remote(src, dst, send, recv, device):
        return pltpu.make_async_remote_copy(
            src_ref=src, dst_ref=dst, send_sem=send, recv_sem=recv,
            device_id=device, device_id_type=MESH,
        )

    def w_copy(k):
        cols = pl.ds(pl.multiple_of(chip(*ROUTES[k][0]) * 2 * BLK, 2 * BLK), 2 * BLK)
        return pltpu.make_async_copy(w_hbm.at[:, cols], w.at[:, cols], w_sem.at[k])

    barrier = pltpu.get_barrier_semaphore()
    for r in PEERS:
        pl.semaphore_signal(barrier, inc=1, device_id=(sec, peer(r)), device_id_type=MESH)
    for other_section in (before, after):
        pl.semaphore_signal(barrier, inc=1, device_id=(other_section, me), device_id_type=MESH)

    g_in = pltpu.make_async_copy(g_hbm, g_ref, in_sem.at[0])
    band_in = pltpu.make_async_copy(band_hbm, band_ref, in_sem.at[1])
    owner_in = pltpu.make_async_copy(owner_hbm, owner_ref, in_sem.at[2])
    g_in.start()
    band_in.start()
    owner_in.start()
    for k in range(CHIPS):
        w_copy(k).start()
    g_in.wait()
    wide = g_ref[...].astype(F32)
    for b in range(BANDS):
        gtok[b] = folded(wide[:, b * BLK:(b + 1) * BLK])[0].astype(BF16)

    pl.semaphore_wait(barrier, DP - 1 + 2)

    def all_of(ref, sem):
        pltpu.make_async_copy(ref, ref, sem).wait()

    def exchange(which, out, into):
        def start():
            for r in PEERS:
                q = peer(r)
                remote(out.at[q], into.at[me], a2a_send.at[which], a2a_recv.at[which], (sec, q)).start()
            into[me] = out[me]

        def recv():
            all_of(into.at[pl.ds(0, DP - 1)], a2a_recv.at[which])

        def sent():
            all_of(out.at[pl.ds(0, DP - 1)], a2a_send.at[which])

        return start, recv, sent

    a_start, a_recv, a_sent = exchange(0, gtok, banded)
    l0_start, l0_recv, l0_sent = exchange(2, l0_out, l0_in)
    r0_start, r0_recv, r0_sent = exchange(3, r0_out, r0_in)
    l1_start, l1_recv, l1_sent = exchange(4, l1_out, l1_in)
    r1_start, r1_recv, r1_sent = exchange(5, r1_out, r1_in)

    a_start()
    band_in.wait()
    owner_in.wait()

    def select(out, source, column):
        for q in range(DP):
            slot = owner_ref[q]
            index = band_ref[column, slot % NB]
            if column == 1:
                index = index + (slot // NB) * BANDS
            out[q] = source[index]

    select(l0_out, gtok, 0)
    l0_start()
    a_recv()
    by_core = banded[...].reshape(CHIPS, CORES, ROWS, HALF)
    for h in range(CORES):
        x0[h] = unfolded(by_core[:, h]).astype(BF16)

    def to_sibling0(h, n):
        pair = pl.ds(2 * n, 2)
        return remote(
            sib_out0.at[h, pair], sib_in0.at[h, pair], sib_send0, sib_recv0.at[h, n], (sec, sibling),
        )

    shared = set()

    def shared0(h, k):
        if (h, k // 2) not in shared:
            shared.add((h, k // 2))
            to_sibling0(h, k // 2).wait_recv()

    def rs0(h, k):
        _, to, slot, _ = ROUTES[k]
        return remote(
            rs_out0.at[h, k], rs_in0.at[h, slot], rs_send0, rs_recv0.at[h, slot],
            (sec, chip(*to) * 2 + core),
        )

    def arrived0(h, slot):
        rs0(h, SENDER[slot]).wait_recv()
        return rs_in0[h, slot].astype(F32)

    def compute0(h, n):
        for k in (2 * n, 2 * n + 1):
            if h == 0:
                w_copy(k).wait()
        for k in (2 * n, 2 * n + 1):
            cols = pl.ds(pl.multiple_of(chip(*ROUTES[k][0]) * 2 * BLK, 2 * BLK), 2 * BLK)
            part = jnp.dot(x0[h], w[:, cols], preferred_element_type=F32)
            sib_out0[h, k] = jnp.where(first, part[:, BLK:], part[:, :BLK]).astype(BF16)
            own0[h, k] = jnp.where(first, part[:, :BLK], part[:, BLK:])
        to_sibling0(h, n).start()

    def finish0(h, *ks):
        for k in ks:
            shared0(h, k)
            for slot in ROUTES[k][3]:
                rs0(h, SENDER[slot]).wait_recv()
        for k in ks:
            total = own0[h, k] + sib_in0[h, k].astype(F32)
            for slot in ROUTES[k][3]:
                total = total + rs_in0[h, slot].astype(F32)
            rs_out0[h, k] = total.astype(BF16)
        for k in ks:
            rs0(h, k).start()

    def band_pass(h):
        return remote(x1_out.at[h], x1.at[h], pass_send.at[h], pass_recv.at[h], (before, me))

    def token_copy(h, c):
        to = chips[CHIP_ORDER[c]]
        return remote(
            n0_out.at[to, h], right0.at[BANDS + me], a2a_send.at[1], a2a_recv.at[1],
            (sec, to * 2 + h),
        )

    def last0(h):
        k = CHIPS - 1
        shared0(h, k)
        total = own0[h, k] + sib_in0[h, k].astype(F32) + x0[h].astype(F32)
        for slot in range(FINAL):
            total = total + arrived0(h, slot)
        x1_out[h] = total.astype(BF16)
        band_pass(h).start()
        n0_out[:, h] = folded(total).astype(BF16)

    def spread(h):
        for c in range(CHIPS - 1):
            token_copy(h, c).start()

        @pl.when(core == h)
        def _():
            right0[BANDS + me] = n0_out[here, h]

        @pl.when(core != h)
        def _():
            token_copy(h, CHIPS - 1).start()

    token_pass = remote(right0.at[pl.ds(BANDS, BANDS)], g1tok, one_send.at[0], one_recv.at[0], (before, me))

    def tokens_on(h):
        @pl.when(core == h)
        def _():
            all_of(right0.at[pl.ds(BANDS, DP - 1)], a2a_recv.at[1])
            token_pass.start()
            if h == 0:
                select(r0_out, right0, 1)
                r0_start()

    def tokens_in(h):
        @pl.when(core == h)
        def _():
            token_pass.wait_recv()

    def to_sibling1(h, j):
        return remote(sib_out1.at[h, j], sib_in1.at[h, j], sib_send1, sib_recv1.at[h, j], (sec, sibling))

    def rs1(h, j, k):
        _, to, slot, _ = ROUTES[k]
        if slot < FINAL:
            return remote(rs_out1.at[h, j, k], fin.at[core, j, slot], rs_send1, fin_recv, (sec, chip(*to) * 2 + h))
        return remote(
            rs_out1.at[h, j, k], rs_in1.at[h, j, slot - FINAL], rs_send1, rs_recv1.at[h, j, slot - FINAL],
            (sec, chip(*to) * 2 + core),
        )

    def arrived1(h, j, slot):
        rs1(h, j, SENDER[slot]).wait_recv()
        return rs_in1[h, j, slot - FINAL].astype(F32)

    def to_owner(j):
        return remote(own_out.at[j], own_in.at[j], one_send.at[1], one_recv.at[1], (sec, sibling))

    def compute1(h, j):
        width = PER * BLK

        def part(c):
            cols = pl.ds(pl.multiple_of(c * SIDE * BLK + j * width, width), width)
            return jnp.dot(x1[h], w[:, cols], preferred_element_type=F32)

        other = part(1 - core)
        for e in range(PER):
            sib_out1[h, j, :, e] = folded(other[:, e * BLK:(e + 1) * BLK]).astype(BF16)
        to_sibling1(h, j).start()
        mine = part(core)
        for e in range(PER):
            own1[h, j, :, e] = folded(mine[:, e * BLK:(e + 1) * BLK])

    def finish1(h, j, ks):
        for k in ks:
            m = chip(*ROUTES[k][0])
            total = own1[h, j, m] + sib_in1[h, j, m].astype(F32)
            for slot in ROUTES[k][3]:
                total = total + arrived1(h, j, slot)
            rs_out1[h, j, k] = total.astype(BF16)
            rs1(h, j, k).start()

    def early1(h, j):
        to_sibling1(h, j).wait_recv()
        finish1(h, j, (0, 1, 2, 3, 4))

        @pl.when(core != h)
        def _():
            own_out[j] = (own1[h, j, here] + sib_in1[h, j, here].astype(F32)).astype(BF16)
            to_owner(j).start()

    def late1(h, j):
        finish1(h, j, (5, 6))

    gout_copy = remote(right1.at[pl.ds(BANDS, BANDS)], gout_in, one_send.at[2], one_recv.at[2], (before, me))

    def last1(h):
        @pl.when(core == h)
        def _():
            all_of(own_in, one_recv.at[1])
            all_of(fin, fin_recv)
            for p in range(CORES):
                for j in range(CHUNKS):
                    at = p * SIDE + j * PER
                    if p == h:
                        total = own1[h, j, here] + sib_in1[h, j, here].astype(F32)
                    else:
                        total = own_in[j].astype(F32)
                    total = total + g1tok[at:at + PER].astype(F32)
                    for slot in range(FINAL):
                        total = total + fin[p, j, slot].astype(F32)
                    right1[BANDS + at:BANDS + at + PER] = total.astype(BF16)
            gout_copy.start()
            select(r1_out, right1, 1)
            r1_start()

    compute0(0, 0)
    compute0(0, 1)
    finish0(0, 0, 1)
    compute0(0, 2)
    finish0(0, 2, 3)
    compute0(0, 3)
    finish0(0, 4)
    compute0(1, 0)
    finish0(0, 5)
    finish0(0, 6)
    compute0(1, 1)
    finish0(1, 0, 1)
    compute0(1, 2)
    finish0(1, 2, 3)
    compute0(1, 3)
    finish0(1, 4)
    last0(0)
    finish0(1, 5)
    finish0(1, 6)
    spread(0)
    right0[:BANDS] = gtok[...]
    band_pass(0).wait_recv()
    compute1(0, 0)
    early1(0, 0)
    last0(1)
    spread(1)
    late1(0, 0)
    tokens_on(0)
    band_pass(1).wait_recv()
    compute1(1, 0)
    early1(1, 0)
    tokens_on(1)
    late1(1, 0)
    tokens_in(0)
    tokens_in(1)
    right1[:BANDS] = g1tok[...]
    last1(0)

    @pl.when(core == 1)
    def _():
        select(r0_out, right0, 1)
        r0_start()

    select(l1_out, g1tok, 0)
    l1_start()
    last1(1)

    def gram(left, right):
        return lax.dot_general(
            unfolded(left).astype(BF16), unfolded(right).astype(BF16),
            (((0,), (0,)), ((), ())), preferred_element_type=F32,
        )

    l0_recv()
    r0_recv()
    l1_recv()
    factors_ref[...] = gram(l0_in[...], r0_in[...])
    gout_copy.wait_recv()
    for b in range(BANDS):
        gout_ref[:, b * BLK:(b + 1) * BLK] = unfolded(gout_in[b:b + 1]).astype(BF16)
    a_sent()
    l0_sent()
    r0_sent()
    l1_sent()
    token_pass.wait_send()
    gout_copy.wait_send()
    all_of(own_out, one_send.at[1])
    all_of(n0_out.at[:CHIPS - 1], a2a_send.at[1])
    all_of(n0_out.at[0, 0], a2a_send.at[1])
    for h in range(CORES):
        band_pass(h).wait_send()
    all_of(sib_out0, sib_send0)
    all_of(rs_out0, rs_send0)
    all_of(sib_out1, sib_send1)
    all_of(rs_out1, rs_send1)
    r1_recv()
    factors_ref[...] = (factors_ref[...] + gram(l1_in[...], r1_in[...])) * (1.0 / (TOKENS * STEPS))

    r1_sent()


def shards(grad_in, weights, band_index, owner):
    vmem = pl.BlockSpec(memory_space=pltpu.VMEM)
    tok = (BANDS, ROWS, HALF)
    dma = pltpu.SemaphoreType.DMA
    factors, gout = pl.pallas_call(
        kernel,
        out_shape=(
            pltpu.VMEM((BLK, BLK), F32),
            pltpu.VMEM((TOK, D), BF16),
        ),
        in_specs=[pl.BlockSpec(memory_space=pl.ANY)] * 4,
        out_specs=(vmem, vmem),
        scratch_shapes=[
            pltpu.VMEM((TOK, D), BF16),
            pltpu.SMEM((2, NB), jnp.int32),
            pltpu.SMEM((DP,), jnp.int32),
            pltpu.VMEM((BLK, D), BF16),
            pltpu.VMEM(tok, BF16),
            pltpu.VMEM(tok, BF16),
            pltpu.VMEM((CORES, ROWS0, BLK), BF16),
            pltpu.VMEM((CORES, ROWS0, BLK), BF16),
            pltpu.VMEM((CORES, ROWS0, BLK), BF16),
            pltpu.VMEM((CORES, CHIPS, ROWS0, BLK), BF16),
            pltpu.VMEM((CORES, CHIPS, ROWS0, BLK), BF16),
            pltpu.VMEM((CORES, CHIPS, ROWS0, BLK), F32),
            pltpu.VMEM((CORES, SLOTS, ROWS0, BLK), BF16),
            pltpu.VMEM((CORES, SLOTS, ROWS0, BLK), BF16),
            pltpu.VMEM((CORES, CHUNKS, CHIPS, PER, ROWS, HALF), BF16),
            pltpu.VMEM((CORES, CHUNKS, CHIPS, PER, ROWS, HALF), BF16),
            pltpu.VMEM((CORES, CHUNKS, CHIPS, PER, ROWS, HALF), F32),
            pltpu.VMEM((CORES, CHUNKS, SLOTS, PER, ROWS, HALF), BF16),
            pltpu.VMEM((CORES, CHUNKS, SLOTS - FINAL, PER, ROWS, HALF), BF16),
            pltpu.VMEM((CHIPS, CORES, ROWS, HALF), BF16),
            pltpu.VMEM((2 * BANDS, ROWS, HALF), BF16),
            pltpu.VMEM(tok, BF16),
            pltpu.VMEM((CHUNKS, PER, ROWS, HALF), BF16),
            pltpu.VMEM((CHUNKS, PER, ROWS, HALF), BF16),
            pltpu.VMEM((CORES, CHUNKS, FINAL, PER, ROWS, HALF), BF16),
            pltpu.VMEM((2 * BANDS, ROWS, HALF), BF16),
            pltpu.VMEM(tok, BF16),
            pltpu.VMEM(tok, BF16),
            pltpu.VMEM(tok, BF16),
            pltpu.VMEM(tok, BF16),
            pltpu.VMEM(tok, BF16),
            pltpu.VMEM(tok, BF16),
            pltpu.VMEM(tok, BF16),
            pltpu.VMEM(tok, BF16),
            pltpu.VMEM(tok, BF16),
            dma((3,)),
            dma((CHIPS,)),
            dma((6,)),
            dma((6,)),
            dma,
            dma((CORES, CHIPS // 2)),
            dma,
            dma((CORES, CHUNKS)),
            dma,
            dma((CORES, SLOTS)),
            dma,
            dma((CORES, CHUNKS, SLOTS - FINAL)),
            dma,
            dma((CORES,)),
            dma((CORES,)),
            dma((3,)),
            dma((3,)),
        ],
        compiler_params=pltpu.CompilerParams(
            collective_id=0, has_side_effects=True, vmem_limit_bytes=58 * 2 ** 20,
        ),
        name="relay",
    )(grad_in[0], weights[0], band_index[0].T, owner)
    return factors[None, None], gout[None]


def solution(mesh):
    return jax.shard_map(
        shards,
        mesh=mesh,
        in_specs=(
            P("section", "dp", None),
            P("section", "dp", None),
            P("section", None, None),
            P(),
        ),
        out_specs=(P("section", "dp", None, None), P("section", "dp", None)),
        check_vma=False,
    )
```
